128 devices in a mesh: ctx: 16 (over y, x), head: 8 (over z, core).
Axes of the slice: x: 4, y: 4, z: 4, core: 2. Of those that a mesh axis runs over, the one named last changes fastest.
Arguments:
- queries: bfloat16 [16384, 8192], P('ctx', 'head'), may hold values from -6 to 6
- keys: bfloat16 [16384, 8192], P('ctx', 'head'), may hold values from -6 to 6
- values: bfloat16 [16384, 8192], P('ctx', 'head'), may hold values from -64 to 64
- gate_logits: bfloat16 [16384, 8192], P('ctx', 'head'), may hold values from -6 to 6
- log_decay: float32 [64, 16384], P('head', 'ctx'), may hold values from 0 to 3, as said below
- norm_gain_vector: float32 [8192], P('head'), may hold values from 0.5 to 1.5
- out_weight: bfloat16 [8192, 6144], P('head'), may hold values from -0.0625 to 0.0625
Outputs:
- layer_out: bfloat16 [16384, 6144], P(('ctx', 'head'))
The draws below stay inside these ranges and needn't reach their ends.
Inputs may be any that keep to these rules, and one draw needn't show every extreme that they name: `log_decay`: log decays are nonnegative.
All inputs are finite; a program needn't handle non-finite values.
Results may differ from the reference program's by a relative error of at most 0.024.
Values may be sent and summed in bfloat16 or wider, within the bound.
A program may use at most 128 MiB of HBM per device.

```python
import math
import jax
import jax.numpy as jnp
from jax import lax

D = 6144
HEADS = 64
HD = 128
BLOCK = 256
TOK_DEV = 1024
TOKENS = 16384
N_HEAD = 8


def draw_values(key, part):
    key = jax.random.fold_in(key, 11)
    first = jax.random.fold_in(key, 0)
    head_of = (jnp.arange(HEADS * HD) // HD).astype(jnp.float32)
    base = jnp.clip(jax.random.normal(first, (TOKENS, HEADS * HD), jnp.float32), -6.0, 6.0)
    scale = jnp.exp(math.log(3.0) * head_of / (HEADS - 1))
    out = base * scale[None, :]
    return out.astype(jnp.bfloat16)


def draw_log_decay(key, part):
    key = jax.random.fold_in(key, 7)
    kind_key, fast_key, jitter_key, seg_key, pos_key, loss_key = jax.random.split(key, 6)
    share = 0.5
    fast = jax.random.uniform(kind_key, (HEADS, 1), jnp.float32) < share
    fast_rate = jnp.exp(jax.random.uniform(fast_key, (HEADS, 1), jnp.float32, math.log(1.0 / 50.0), math.log(1.0 / 30.0)))
    decay_speed = jnp.where(fast, fast_rate, 0.3 / TOKENS)
    random_noise = jnp.exp(jax.random.uniform(jitter_key, (HEADS, TOKENS), jnp.float32, math.log(0.5), math.log(2.0)))
    segment_span = jnp.exp(jax.random.uniform(seg_key, (HEADS, TOKENS // TOK_DEV), jnp.float32, math.log(0.5), math.log(2.0)))
    segment_span = jnp.repeat(segment_span, TOK_DEV, axis=1)
    spots = jax.random.randint(pos_key, (HEADS, 3), 0, TOKENS)
    decay_falloff = jax.random.uniform(loss_key, (HEADS, 3), jnp.float32, 0.22, 0.69)
    match_tally = (jnp.arange(TOKENS)[None, None, :] == spots[:, :, None]).astype(jnp.float32)
    spike_amount = jnp.sum(match_tally * decay_falloff[:, :, None], axis=1)
    return (decay_speed * random_noise * segment_span + spike_amount).astype(jnp.float32)


def block_scale(rng, shape, shards, smallest, high):
    gain, own = 1.0, jax.random.fold_in(rng, 6)
    for dim, parts in shards:
        heights = jnp.exp(jax.random.uniform(jax.random.fold_in(own, dim), (parts,), jnp.float32, smallest / len(shards), high / len(shards)))
        gain = gain * jnp.repeat(heights, shape[dim] // parts).reshape([-1 if axis == dim else 1 for axis in range(len(shape))])
    return gain


def scatter_about(own_key, dims, scale, reach, cuts=(), kind=jnp.bfloat16):
    array = scale * jax.random.normal(own_key, dims, jnp.float32)
    if cuts:
        array = array * block_scale(own_key, dims, cuts, -0.22, 0.18)
    return jnp.clip(array, -reach, reach).astype(kind)


def setup_inputs(seed: int = 0) -> dict:
    key_list = jax.random.split(jax.random.key(seed), 8)
    queries = scatter_about(key_list[0], (TOKENS, HEADS * HD), 1.0, 6.0, ((0, 16), (1, 8)))
    keys = scatter_about(key_list[1], (TOKENS, HEADS * HD), 1.0, 6.0, ((0, 16), (1, 8)))
    values = draw_values(jax.random.fold_in(key_list[7], 71), 0)
    gate_logits = scatter_about(key_list[3], (TOKENS, HEADS * HD), 1.0, 6.0, ((0, 16), (1, 8)))
    log_decay = draw_log_decay(jax.random.fold_in(key_list[7], 71), 0)
    norm_gain_vector = jnp.clip(1.0 + 0.1 * jax.random.normal(key_list[5], (HEADS * HD,), jnp.float32), 0.5, 1.5)
    out_weight = scatter_about(key_list[6], (HEADS * HD, D), (HEADS * HD) ** -0.5, 0.0625, ((0, 8),))
    return dict(queries=queries, keys=keys, values=values, gate_logits=gate_logits, log_decay=log_decay, norm_gain_vector=norm_gain_vector, out_weight=out_weight)


def reference(queries, keys, values, gate_logits, log_decay, norm_gain_vector, out_weight):
    blocks = TOKENS // BLOCK
    hi = lax.Precision.HIGHEST
    qq = queries.reshape(blocks, BLOCK, HEADS, HD).transpose(0, 2, 1, 3)
    kk = keys.reshape(blocks, BLOCK, HEADS, HD).transpose(0, 2, 1, 3)
    vv = values.reshape(blocks, BLOCK, HEADS, HD).transpose(0, 2, 1, 3)
    decays = log_decay.reshape(HEADS, blocks, BLOCK).transpose(1, 0, 2)
    lower = jnp.arange(BLOCK)[:, None] >= jnp.arange(BLOCK)[None, :]
    lowerf = lower.astype(jnp.float32)

    def advance(state, inputs):
        qb, kb, vb, gb = inputs
        cum = jnp.einsum('hj,ij->hi', gb, lowerf, precision=hi)
        diff = cum[:, :, None] - cum[:, None, :]
        decay = jnp.where(lower[None], jnp.exp(-jnp.where(lower[None], diff, 0.0)), 0.0)
        scores = jnp.einsum('hid,hjd->hij', qb.astype(jnp.float32), kb.astype(jnp.float32))
        weights = (scores * decay).astype(jnp.bfloat16)
        intra = jnp.einsum('hij,hjd->hid', weights.astype(jnp.float32), vb.astype(jnp.float32))
        qdec = (qb.astype(jnp.float32) * jnp.exp(-cum)[:, :, None]).astype(jnp.bfloat16)
        inter = jnp.einsum('hid,hde->hie', qdec.astype(jnp.float32), state.astype(jnp.bfloat16).astype(jnp.float32))
        last = cum[:, -1:]
        kdec = (kb.astype(jnp.float32) * jnp.exp(-(last - cum))[:, :, None]).astype(jnp.bfloat16)
        update = jnp.einsum('hjd,hje->hde', kdec.astype(jnp.float32), vb.astype(jnp.float32))
        state = jnp.exp(-last[:, 0])[:, None, None] * state + update
        return (state, intra + inter)
    start = jnp.zeros((HEADS, HD, HD), jnp.float32)
    final, outs = lax.scan(advance, start, (qq, kk, vv, decays))
    attn = outs.transpose(0, 2, 1, 3).reshape(TOKENS, HEADS * HD)
    scale = lax.rsqrt(lax.optimization_barrier(jnp.mean(attn * attn, axis=1)) + 1e-06)
    hidden = (attn * scale[:, None] * norm_gain_vector[None, :] * jax.nn.sigmoid(gate_logits.astype(jnp.float32))).astype(jnp.bfloat16)
    group = HEADS // N_HEAD * HD
    total = jnp.zeros((TOKENS, D), jnp.float32)
    for index in range(N_HEAD):
        part_cols = hidden[:, index * group:(index + 1) * group]
        part_rows = out_weight[index * group:(index + 1) * group]
        term = jnp.dot(part_cols, part_rows, preferred_element_type=jnp.float32).astype(jnp.bfloat16)
        total = total + term.astype(jnp.float32)
    return total.astype(jnp.bfloat16)
```

```python
import functools

import jax
import jax.numpy as jnp
from jax import lax
from jax.experimental import pallas as pl
from jax.experimental.pallas import tpu as pltpu
from jax.sharding import PartitionSpec as P

HEADS = 64
HD = 128
BLOCK = 256
EPS = 1e-06

N_CTX = 16
N_HEAD = 8
ROWS = 1024
WIDTH = 1024
D = 6144
LH = 8
NB = 4
HALF = 128
CN = 512
NC = D // CN
NH = NC // 2
SL = LH * HD // N_CTX
MSG = SL + 16

F32 = jnp.float32
BF16 = jnp.bfloat16
HI = lax.Precision.HIGHEST


def ds(start, size):
    return pl.ds(pl.multiple_of(start * size, size), size)


def kernel(
    q_hbm, k_hbm, v_hbm, gate_hbm, decay_ref, gain_ref, w_hbm, out_hbm,
    q_v, k_v, v_v, gate_v, w_v, hid, intra, gated, local, cur,
    cum_row, cum_col, dec_col, before_dec,
    scan_out, scan_in, prefix_out, prefix_in, ssq_out, ssq_in,
    core_out, core_in, own, z_out, far_in, near_in, total, out_v,
    load_sem, w_sem, out_sem, scan_ssem, scan_rsem, pre_ssem, pre_rsem,
    ssq_ssem, ssq_rsem, core_ssem, core_rsem, z_ssem, far_rsem, near_rsem,
):
    ctx = lax.axis_index("ctx")
    head = lax.axis_index("head")
    z = head // 2
    core = head % 2
    partner = z * 2 + (1 - core)
    zr = (z + 1) % 4
    zl = (z + 3) % 4
    zo = (z + 2) % 4
    right = zr * 2 + core
    left = zl * 2 + core

    def load(src, dst, sem):
        return pltpu.make_async_copy(src, dst, sem)

    def block_load(i, src, dst, b):
        return load(src.at[ds(b, BLOCK)], dst.at[ds(b, BLOCK)], load_sem.at[i, b])

    def w_load(n):
        return load(w_hbm.at[:, ds(n, CN)], w_v.at[n], w_sem.at[n])

    for b in range(NB):
        block_load(0, k_hbm, k_v, b).start()
        block_load(1, v_hbm, v_v, b).start()

    barrier = pltpu.get_barrier_semaphore()

    def greet_ctx(d, _):
        pl.semaphore_signal(barrier, inc=1, device_id={"ctx": (ctx + d) % N_CTX},
                            device_id_type=pl.DeviceIdType.MESH)
        return 0

    def greet_head(d, _):
        pl.semaphore_signal(barrier, inc=1, device_id={"head": (head + d) % N_HEAD},
                            device_id_type=pl.DeviceIdType.MESH)
        return 0

    lax.fori_loop(1, N_CTX, greet_ctx, 0)
    lax.fori_loop(1, N_HEAD, greet_head, 0)

    for b in range(NB):
        block_load(2, q_hbm, q_v, b).start()

    ri = lax.broadcasted_iota(jnp.int32, (BLOCK, BLOCK), 0)
    ci = lax.broadcasted_iota(jnp.int32, (BLOCK, BLOCK), 1)
    lower = (ri >= ci).astype(F32)
    nt = (((1,), (1,)), ((), ()))
    tn = (((0,), (0,)), ((), ()))
    before = jnp.zeros((1, LH), F32)
    for b in range(NB):
        dec = decay_ref[:, b * BLOCK:(b + 1) * BLOCK]
        row = lax.dot_general(dec, lower, nt, precision=HI, preferred_element_type=F32)
        col = lax.dot_general(lower, dec, nt, precision=HI, preferred_element_type=F32)
        cum_row[b] = row
        cum_col[b] = col
        dec_col[b] = jnp.exp(-col)
        before_dec[b, 0:1, :] = jnp.exp(-before)
        before = before + col[BLOCK - 1:BLOCK, :]
    shard_dec = jnp.exp(-before)

    cur[...] = jnp.zeros_like(cur)

    def update(b, _):
        block_load(0, k_hbm, k_v, b).wait()
        block_load(1, v_hbm, v_v, b).wait()
        col = cum_col[b]
        last = col[BLOCK - 1:BLOCK, :]
        factor = jnp.exp(col - last)
        carry = jnp.exp(-last)
        for h in range(LH):
            kb = k_v[ds(b, BLOCK), h * HD:(h + 1) * HD].astype(F32)
            vb = v_v[ds(b, BLOCK), h * HD:(h + 1) * HD]
            kd = (kb * factor[:, h:h + 1]).astype(BF16)
            new = lax.dot_general(kd, vb, tn, preferred_element_type=F32)
            old = cur[h]
            local[b, h] = old
            cur[h] = carry[:, h:h + 1] * old + new
        return 0

    lax.fori_loop(0, NB, update, 0)

    tile = lax.broadcasted_iota(jnp.int32, (16, HD), 0)
    for h in range(LH):
        a = jnp.broadcast_to(shard_dec[:, h:h + 1], (16, HD))
        hi = a.astype(BF16).astype(F32)
        mid = (a - hi).astype(BF16).astype(F32)
        low = a - hi - mid
        parts = jnp.where(tile == 0, hi, jnp.where(tile == 1, mid, jnp.where(tile == 2, low, 0.0)))
        parts = parts.astype(BF16)
        for s in range(2):
            scan_out[2 * h + s, 0:SL] = cur[h, s * SL:(s + 1) * SL].astype(BF16)
            scan_out[2 * h + s, SL:MSG] = parts

    pl.semaphore_wait(barrier, N_CTX - 1 + N_HEAD - 1)

    def scan_copy(there, slot):
        return pltpu.make_async_remote_copy(
            src_ref=scan_out.at[there], dst_ref=scan_in.at[slot],
            send_sem=scan_ssem.at[there], recv_sem=scan_rsem.at[slot],
            device_id={"ctx": there}, device_id_type=pl.DeviceIdType.MESH)

    def prefix_copy(there, slot):
        return pltpu.make_async_remote_copy(
            src_ref=prefix_out.at[there], dst_ref=prefix_in.at[slot],
            send_sem=pre_ssem.at[there], recv_sem=pre_rsem.at[slot],
            device_id={"ctx": there}, device_id_type=pl.DeviceIdType.MESH)

    def scan_send(d, _):
        scan_copy((ctx + d) % N_CTX, ctx).start()
        return 0

    lax.fori_loop(1, N_CTX, scan_send, 0)
    scan_in[ctx] = scan_out[ctx]

    for j in range(NH):
        w_load(j).start()
        w_load(NH + j).start()
    for b in range(NB):
        block_load(3, gate_hbm, gate_v, b).start()

    r2 = lax.broadcasted_iota(jnp.int32, (HALF, HALF), 0)
    c2 = lax.broadcasted_iota(jnp.int32, (HALF, HALF), 1)
    keep = r2 >= c2

    def inside(b, _):
        block_load(2, q_hbm, q_v, b).wait()
        rows = cum_row[b]
        cols = cum_col[b]
        for h in range(LH):
            lanes = slice(h * HD, (h + 1) * HD)
            qb = q_v[ds(b, BLOCK), lanes]
            kb = k_v[ds(b, BLOCK), lanes]
            vb = v_v[ds(b, BLOCK), lanes]
            scores = lax.dot_general(qb, kb, nt, preferred_element_type=F32)
            cr = rows[h:h + 1, :]
            cc = jnp.broadcast_to(cols[:, h:h + 1], (BLOCK, HALF))
            top = jnp.where(keep, scores[:HALF, :HALF] * jnp.exp(cr[:, :HALF] - cc[:HALF]), 0.0)
            bl = scores[HALF:, :HALF] * jnp.exp(cr[:, :HALF] - cc[HALF:])
            br = jnp.where(keep, scores[HALF:, HALF:] * jnp.exp(cr[:, HALF:] - cc[HALF:]), 0.0)
            a0 = jnp.dot(top.astype(BF16), vb[:HALF], preferred_element_type=F32)
            bottom = jnp.concatenate([bl.astype(BF16), br.astype(BF16)], axis=1)
            a1 = jnp.dot(bottom, vb, preferred_element_type=F32)
            intra[b, :HALF, lanes] = a0
            intra[b, HALF:, lanes] = a1
        return 0

    lax.fori_loop(0, 2, inside, 0)

    def prefix(s, state):
        @pl.when(s != ctx)
        def _():
            scan_copy(ctx, s).wait_recv()

        prefix_out[s] = state.astype(BF16)

        @pl.when(s != ctx)
        def _():
            prefix_copy(s, ctx).start()

        dec = jnp.sum(scan_in[s, SL:MSG].astype(F32), axis=0, keepdims=True)
        return dec * state + scan_in[s, 0:SL].astype(F32)

    lax.fori_loop(0, N_CTX, prefix, jnp.zeros((SL, HD), F32))
    prefix_in[ctx] = prefix_out[ctx]

    lax.fori_loop(2, NB, inside, 0)

    def gating(b, _):
        block_load(3, gate_hbm, gate_v, b).wait()
        for h in range(LH):
            lanes = slice(h * HD, (h + 1) * HD)
            gl = gate_v[ds(b, BLOCK), lanes].astype(F32)
            gated[b, :, lanes] = jax.nn.sigmoid(gl) * gain_ref[:, lanes]
        return 0

    lax.fori_loop(0, NB, gating, 0)

    def prefix_wait(d, _):
        prefix_copy(ctx, (ctx + d) % N_CTX).wait_recv()
        return 0

    lax.fori_loop(1, N_CTX, prefix_wait, 0)

    ones = jnp.ones((8, HD), F32)

    def ssq_copy(there, slot):
        return pltpu.make_async_remote_copy(
            src_ref=ssq_out.at[there], dst_ref=ssq_in.at[slot],
            send_sem=ssq_ssem.at[there], recv_sem=ssq_rsem.at[slot],
            device_id={"head": there}, device_id_type=pl.DeviceIdType.MESH)

    def finish(rb):
        dc = dec_col[rb]
        bd = before_dec[rb]
        square = jnp.zeros((BLOCK, HD), F32)
        for h in range(LH):
            lanes = slice(h * HD, (h + 1) * HD)
            carried = jnp.concatenate([prefix_in[2 * h], prefix_in[2 * h + 1]], axis=0)
            start = (bd[0:1, h:h + 1] * carried.astype(F32) + local[rb, h]).astype(BF16)
            inter = jnp.dot(q_v[ds(rb, BLOCK), lanes], start, preferred_element_type=F32)
            attn = intra[rb, :, lanes] + dc[:, h:h + 1] * inter
            square = square + attn * attn
            hidden = (attn * gated[rb, :, lanes]).astype(BF16)
            hid[rb, ds(1 - core, HALF), lanes] = hidden[:HALF]
            hid[rb, ds(core, HALF), lanes] = hidden[HALF:]
        sums = lax.dot_general(ones, square, nt, precision=HI, preferred_element_type=F32)
        for s in range(2):
            there = rb * 2 + s
            ssq_out[there] = sums[:, s * HALF:(s + 1) * HALF]

            @pl.when(there != head)
            def _():
                ssq_copy(there, head).start()

            @pl.when(there == head)
            def _():
                ssq_in[head] = ssq_out[head]

    def core_copy(slot):
        return pltpu.make_async_remote_copy(
            src_ref=core_out.at[slot], dst_ref=core_in.at[slot],
            send_sem=core_ssem.at[slot], recv_sem=core_rsem.at[slot],
            device_id={"head": partner}, device_id_type=pl.DeviceIdType.MESH)

    def far_copy(n, there):
        return pltpu.make_async_remote_copy(
            src_ref=z_out.at[0, n], dst_ref=far_in.at[n],
            send_sem=z_ssem.at[0, n], recv_sem=far_rsem.at[n],
            device_id={"head": there}, device_id_type=pl.DeviceIdType.MESH)

    def near_copy(side, n, there):
        return pltpu.make_async_remote_copy(
            src_ref=z_out.at[1 + side, n], dst_ref=near_in.at[side, n],
            send_sem=z_ssem.at[1 + side, n], recv_sem=near_rsem.at[side, n],
            device_id={"head": there}, device_id_type=pl.DeviceIdType.MESH)

    def product(phase, lane, rb, n):
        slot = phase * NC + n
        r = jnp.dot(hid[rb], w_v[n], preferred_element_type=F32)
        core_out[slot] = r[:HALF].astype(BF16)
        core_copy(slot).start()
        return r[HALF:]

    def summed(phase, lane, n):
        slot = phase * NC + n
        core_copy(slot).wait_recv()
        return own[lane] + core_in[slot].astype(F32)

    def fin0(lane, j):
        n = lane * NH + j
        z_out[0, n] = summed(0, lane, n).astype(BF16)
        far_copy(n, right if lane == 0 else left).start()

    def fin1(lane, j):
        n = (1 - lane) * NH + j
        z_out[1 + lane, n] = summed(1, lane, n).astype(BF16)
        near_copy(lane, n, right if lane == 0 else left).start()

    def fin2(lane, j):
        n = lane * NH + j
        s = summed(2, lane, n)
        far_copy(n, right if lane == 0 else left).wait_recv()
        z_out[1 + lane, n] = (s + far_in[n].astype(F32)).astype(BF16)
        near_copy(lane, n, right if lane == 0 else left).start()

    def fin3(lane, j):
        n = lane * NH + j
        total[n] = summed(3, lane, n)

    def step(phase, lane, j):
        n = (1 - lane) * NH + j if phase == 1 else lane * NH + j
        if phase == 0:
            rb = zo
        elif phase == 3:
            rb = z
        else:
            rb = zr if lane == 0 else zl
        if phase == 0:
            w_load(n).wait()
        return product(phase, lane, rb, n)

    fins = (fin0, fin1, fin2, fin3)
    pending = None
    for phase in range(4):
        if phase == 0:
            finish(zo)
        elif phase == 1:
            finish(zr)
            finish(zl)
        elif phase == 3:
            finish(z)
        for lane in range(2):
            r = step(phase, lane, 0)
            if pending is not None:
                pending(lane, NH - 1)
            own[lane] = r

        def body(j, _, phase=phase):
            for lane in range(2):
                r = step(phase, lane, j)
                fins[phase](lane, j - 1)
                own[lane] = r
            return 0

        lax.fori_loop(1, NH, body, 0)
        pending = fins[phase]
    for lane in range(2):
        pending(lane, NH - 1)

    def ssq_wait(d, _):
        ssq_copy(head, (head + d) % N_HEAD).wait_recv()
        return 0

    lax.fori_loop(1, N_HEAD, ssq_wait, 0)
    squares = jnp.sum(ssq_in[...], axis=0)
    scale_row = lax.rsqrt(squares[0:1, :] * (1.0 / (HEADS * HD)) + EPS)
    scale = jnp.sum(
        jnp.where(r2 == c2, jnp.broadcast_to(scale_row, (HALF, HALF)), 0.0), axis=1, keepdims=True)

    def out_copy(n):
        return load(out_v.at[n], out_hbm.at[:, ds(n, CN)], out_sem.at[n])

    def result(j, _):
        for lane in range(2):
            n = lane * NH + j
            near_copy(0, n, right).wait_recv()
            near_copy(1, n, left).wait_recv()
            s = total[n] + near_in[0, n].astype(F32) + near_in[1, n].astype(F32)
            out_v[n] = (s * scale).astype(BF16)
            out_copy(n).start()
        return 0

    lax.fori_loop(0, NH, result, 0)

    def drain_scan(d, _):
        scan_copy((ctx + d) % N_CTX, ctx).wait_send()
        prefix_copy((ctx + d) % N_CTX, ctx).wait_send()
        return 0

    def drain_ssq(d, _):
        ssq_copy((head + d) % N_HEAD, head).wait_send()
        return 0

    def drain_core(s, _):
        core_copy(s).wait_send()
        return 0

    def drain_z(n, _):
        far_copy(n, right).wait_send()
        near_copy(0, n, right).wait_send()
        near_copy(1, n, left).wait_send()
        return 0

    lax.fori_loop(1, N_CTX, drain_scan, 0)
    lax.fori_loop(1, N_HEAD, drain_ssq, 0)
    lax.fori_loop(0, 4 * NC, drain_core, 0)
    lax.fori_loop(0, NC, drain_z, 0)

    def drain_out(n, _):
        out_copy(n).wait()
        return 0

    lax.fori_loop(0, NC, drain_out, 0)


def shards(queries, keys, values, gate_logits, log_decay, norm_gain_vector, out_weight):
    any_spec = pl.BlockSpec(memory_space=pl.ANY)
    vmem = pl.BlockSpec(memory_space=pltpu.VMEM)
    dma = pltpu.SemaphoreType.DMA
    return pl.pallas_call(
        kernel,
        out_shape=jax.ShapeDtypeStruct((ROWS // N_HEAD, D), BF16),
        in_specs=[any_spec] * 4 + [vmem, vmem, any_spec],
        out_specs=any_spec,
        scratch_shapes=[
            pltpu.VMEM((ROWS, WIDTH), BF16),
            pltpu.VMEM((ROWS, WIDTH), BF16),
            pltpu.VMEM((ROWS, WIDTH), BF16),
            pltpu.VMEM((ROWS, WIDTH), BF16),
            pltpu.VMEM((NC, WIDTH, CN), BF16),
            pltpu.VMEM((NB, BLOCK, WIDTH), BF16),
            pltpu.VMEM((NB, BLOCK, WIDTH), F32),
            pltpu.VMEM((NB, BLOCK, WIDTH), F32),
            pltpu.VMEM((NB, LH, HD, HD), F32),
            pltpu.VMEM((LH, HD, HD), F32),
            pltpu.VMEM((NB, LH, BLOCK), F32),
            pltpu.VMEM((NB, BLOCK, LH), F32),
            pltpu.VMEM((NB, BLOCK, LH), F32),
            pltpu.VMEM((NB, 8, LH), F32),
            pltpu.VMEM((N_CTX, MSG, HD), BF16),
            pltpu.VMEM((N_CTX, MSG, HD), BF16),
            pltpu.VMEM((N_CTX, SL, HD), BF16),
            pltpu.VMEM((N_CTX, SL, HD), BF16),
            pltpu.VMEM((N_HEAD, 8, HALF), F32),
            pltpu.VMEM((N_HEAD, 8, HALF), F32),
            pltpu.VMEM((4 * NC, HALF, CN), BF16),
            pltpu.VMEM((4 * NC, HALF, CN), BF16),
            pltpu.VMEM((2, HALF, CN), F32),
            pltpu.VMEM((3, NC, HALF, CN), BF16),
            pltpu.VMEM((NC, HALF, CN), BF16),
            pltpu.VMEM((2, NC, HALF, CN), BF16),
            pltpu.VMEM((NC, HALF, CN), F32),
            pltpu.VMEM((NC, HALF, CN), BF16),
            dma((4, NB)), dma((NC,)), dma((NC,)),
            dma((N_CTX,)), dma((N_CTX,)), dma((N_CTX,)), dma((N_CTX,)),
            dma((N_HEAD,)), dma((N_HEAD,)),
            dma((4 * NC,)), dma((4 * NC,)),
            dma((3, NC)), dma((NC,)), dma((2, NC)),
        ],
        compiler_params=pltpu.CompilerParams(
            collective_id=0, has_side_effects=True, vmem_limit_bytes=63 * 1024 * 1024),
        cost_estimate=pl.CostEstimate(
            flops=15_000_000_000, bytes_accessed=23_000_000, transcendentals=4_000_000),
        name="attention",
    )(queries, keys, values, gate_logits, log_decay, norm_gain_vector.reshape(1, WIDTH), out_weight)


def solution(mesh):
    in_specs = (
        P("ctx", "head"),
        P("ctx", "head"),
        P("ctx", "head"),
        P("ctx", "head"),
        P("head", "ctx"),
        P("head"),
        P("head", None),
    )
    out_specs = P(("ctx", "head"), None)
    return jax.shard_map(shards, mesh=mesh, in_specs=in_specs, out_specs=out_specs, check_vma=False)
```

```python
import functools

import jax
import jax.numpy as jnp
from jax import lax
from jax.experimental import pallas as pl
from jax.experimental.pallas import tpu as pltpu
from jax.sharding import PartitionSpec as P

HEADS = 64
HD = 128
BLOCK = 256
EPS = 1e-06

N_CTX = 16
N_HEAD = 8
ROWS = 1024
WIDTH = 1024
D = 6144
LH = 8
NB = 4
HALF = 128
PAIR = 2 * HD
CN = 512
NC = D // CN
NH = NC // 2
SL = LH * HD // N_CTX
MSG = SL + 16

F32 = jnp.float32
BF16 = jnp.bfloat16
HI = lax.Precision.HIGHEST


def ds(start, size):
    return pl.ds(pl.multiple_of(start * size, size), size)


def kernel(
    q_hbm, k_hbm, v_hbm, gate_hbm, decay_hbm, gain_hbm, w_hbm, out_ref,
    decay_ref, gain_ref,
    q_v, k_v, v_v, gate_v, w_v, hid, intra, gated, local,
    cum_row, cum_col, dec_col, before_dec, factor, keep_dec, parts,
    scan_out, scan_in, prefix_out, prefix_in, ssq_out, ssq_in,
    core_out, core_in, own, z_out, far_in, near_in,
    load_sem, once_sem, scan_sem, core_ssem, core_rsem, z_ssem, far_rsem, early_rsem, late_rsem,
):
    ctx = lax.axis_index("ctx")
    head = lax.axis_index("head")
    z = head // 2
    core = head % 2
    partner = z * 2 + (1 - core)
    zr = (z + 1) % 4
    zl = (z + 3) % 4
    zo = (z + 2) % 4
    right = zr * 2 + core
    left = zl * 2 + core

    def load(src, dst, sem):
        return pltpu.make_async_copy(src, dst, sem)

    def block_load(i, src, dst, b):
        return load(src.at[ds(b, BLOCK)], dst.at[ds(b, BLOCK)], load_sem.at[i, b])

    def w_load(n):
        return load(w_hbm.at[:, ds(n, CN)], w_v.at[n], once_sem.at[4])

    q_load = load(q_hbm, q_v, once_sem.at[0])
    gate_load = load(gate_hbm, gate_v, once_sem.at[1])
    decay_load = load(decay_hbm, decay_ref, once_sem.at[2])
    gain_load = load(gain_hbm, gain_ref, once_sem.at[3])
    decay_load.start()

    def all_of(ref, sem):
        load(ref, ref, sem).wait()

    ctx_y = ctx // 4
    ctx_x = ctx % 4
    far_first = (2, 1, 3, 0)
    pairs = [(ctx_y + off) % 4 for off in far_first]
    for b in range(NB):
        block_load(0, k_hbm, k_v, b).start()
        block_load(1, v_hbm, v_v, b).start()

    barrier = pltpu.get_barrier_semaphore()

    def greet_ctx(d, _):
        pl.semaphore_signal(barrier, inc=1, device_id={"ctx": (ctx + d) % N_CTX},
                            device_id_type=pl.DeviceIdType.MESH)
        return 0

    def greet_head(d, _):
        pl.semaphore_signal(barrier, inc=1, device_id={"head": (head + d) % N_HEAD},
                            device_id_type=pl.DeviceIdType.MESH)
        return 0

    lax.fori_loop(1, N_CTX, greet_ctx, 0)
    lax.fori_loop(1, N_HEAD, greet_head, 0)

    ri = lax.broadcasted_iota(jnp.int32, (BLOCK, BLOCK), 0)
    ci = lax.broadcasted_iota(jnp.int32, (BLOCK, BLOCK), 1)
    lower = (ri >= ci).astype(F32)
    eye = (ri == ci).astype(BF16)
    nt = (((1,), (1,)), ((), ()))
    before = jnp.zeros((LH, 1), F32)
    decay_load.wait()
    tile = lax.broadcasted_iota(jnp.int32, (16, HD), 0)
    for b in range(NB):
        dec = decay_ref[:, b * BLOCK:(b + 1) * BLOCK]
        row = lax.dot_general(dec, lower, nt, precision=HI, preferred_element_type=F32)
        cum_row[b] = row
        last = row[:, BLOCK - 1:BLOCK]
        fac = jnp.exp(row - last)
        kept = jnp.broadcast_to(jnp.exp(-last), (LH, HD))
        before_dec[b] = jnp.broadcast_to(jnp.exp(-before), (LH, HD))
        before = before + last
        for p in range(4):
            factor[b, p] = fac[2 * p:2 * p + 2]
            keep_dec[b, p] = kept[2 * p:2 * p + 2]
    shard_dec = jnp.broadcast_to(jnp.exp(-before), (LH, HD))
    for h in range(LH):
        a = jnp.broadcast_to(shard_dec[h:h + 1], (16, HD))
        hi = a.astype(BF16).astype(F32)
        mid = (a - hi).astype(BF16).astype(F32)
        low = a - hi - mid
        part = jnp.where(tile == 0, hi, jnp.where(tile == 1, mid, jnp.where(tile == 2, low, 0.0)))
        parts[h // 2, h % 2] = part.astype(BF16)

    def scan_copy(there, slot):
        return pltpu.make_async_remote_copy(
            src_ref=scan_out.at[there], dst_ref=scan_in.at[slot],
            send_sem=scan_sem.at[0], recv_sem=scan_sem.at[1],
            device_id={"ctx": there}, device_id_type=pl.DeviceIdType.MESH)

    def prefix_copy(there, slot):
        return pltpu.make_async_remote_copy(
            src_ref=prefix_out.at[there], dst_ref=prefix_in.at[slot],
            send_sem=scan_sem.at[2], recv_sem=scan_sem.at[3],
            device_id={"ctx": there}, device_id_type=pl.DeviceIdType.MESH)

    def added(b, p):
        rows = slice(b * BLOCK, (b + 1) * BLOCK)
        lanes = ds(p, PAIR)
        flipped = lax.dot_general(eye, k_v[rows, lanes], nt, preferred_element_type=F32)
        vb = v_v[rows, lanes]
        new = []
        for s in range(2):
            kd = (flipped[s * HD:(s + 1) * HD] * factor[b, p, s:s + 1, :]).astype(BF16)
            new.append(jnp.dot(kd, vb[:, s * HD:(s + 1) * HD], preferred_element_type=F32))
        return new

    for b in range(NB - 1):
        block_load(0, k_hbm, k_v, b).wait()
        block_load(1, v_hbm, v_v, b).wait()
        for p in range(4):
            for s, new in enumerate(added(b, p)):
                if b == 0:
                    local[0, p, s] = jnp.zeros((HD, HD), F32)
                else:
                    new = new + keep_dec[b, p, s:s + 1, :] * local[b, p, s]
                local[b + 1, p, s] = new

    block_load(0, k_hbm, k_v, NB - 1).wait()
    block_load(1, v_hbm, v_v, NB - 1).wait()
    q_load.start()

    for i, p in enumerate(pairs):
        for s, new in enumerate(added(NB - 1, p)):
            state = new + keep_dec[NB - 1, p, s:s + 1, :] * local[NB - 1, p, s]
            for t in range(2):
                scan_out[4 * p + 2 * s + t, 0:SL] = state[t * SL:(t + 1) * SL].astype(BF16)
                scan_out[4 * p + 2 * s + t, SL:MSG] = parts[p, s]
        if i == 0:
            pl.semaphore_wait(barrier, N_CTX - 1 + N_HEAD - 1)
        for off in far_first:
            there = 4 * p + (ctx_x + off) % 4
            if far_first[i] == 0 and off == 0:
                scan_in[ctx] = scan_out[ctx]
            else:
                scan_copy(there, ctx).start()

    for j in range(NH):
        w_load(j).start()
        w_load(NH + j).start()
    gate_load.start()
    gain_load.start()

    for b in range(NB):
        dec = decay_ref[:, b * BLOCK:(b + 1) * BLOCK]
        col = lax.dot_general(lower, dec, nt, precision=HI, preferred_element_type=F32)
        cum_col[b] = col
        dec_col[b] = jnp.exp(-col)

    r2 = lax.broadcasted_iota(jnp.int32, (HALF, HALF), 0)
    c2 = lax.broadcasted_iota(jnp.int32, (HALF, HALF), 1)
    keep = r2 >= c2

    def inside(b, _):
        rows = cum_row[b]
        cols = cum_col[b]
        for h in range(LH):
            lanes = slice(h * HD, (h + 1) * HD)
            qb = q_v[ds(b, BLOCK), lanes]
            kb = k_v[ds(b, BLOCK), lanes]
            vb = v_v[ds(b, BLOCK), lanes]
            scores = lax.dot_general(qb, kb, nt, preferred_element_type=F32)
            cr = rows[h:h + 1, :]
            cc = jnp.broadcast_to(cols[:, h:h + 1], (BLOCK, HALF))
            top = jnp.where(keep, scores[:HALF, :HALF] * jnp.exp(cr[:, :HALF] - cc[:HALF]), 0.0)
            bl = scores[HALF:, :HALF] * jnp.exp(cr[:, :HALF] - cc[HALF:])
            br = jnp.where(keep, scores[HALF:, HALF:] * jnp.exp(cr[:, HALF:] - cc[HALF:]), 0.0)
            a0 = jnp.dot(top.astype(BF16), vb[:HALF], preferred_element_type=F32)
            bottom = jnp.concatenate([bl.astype(BF16), br.astype(BF16)], axis=1)
            a1 = jnp.dot(bottom, vb, preferred_element_type=F32)
            intra[b, :HALF, lanes] = a0
            intra[b, HALF:, lanes] = a1
        return 0

    q_load.wait()
    lax.fori_loop(0, 2, inside, 0)

    def prefix(s, state):
        prefix_out[s] = state.astype(BF16)
        dec = jnp.sum(scan_in[s, SL:MSG].astype(F32), axis=0, keepdims=True)
        return dec * state + scan_in[s, 0:SL].astype(F32)

    all_of(scan_in.at[0:N_CTX - 1], scan_sem.at[1])
    lax.fori_loop(0, N_CTX, prefix, jnp.zeros((SL, HD), F32))
    for dy in far_first:
        for dx in far_first:
            if dy == 0 and dx == 0:
                prefix_in[ctx] = prefix_out[ctx]
            else:
                prefix_copy((ctx_y + dy) % 4 * 4 + (ctx_x + dx) % 4, ctx).start()

    lax.fori_loop(2, NB, inside, 0)

    def gating(b, _):
        for h in range(LH):
            lanes = slice(h * HD, (h + 1) * HD)
            gl = gate_v[ds(b, BLOCK), lanes].astype(F32)
            gated[b, :, lanes] = jax.nn.sigmoid(gl) * gain_ref[:, lanes]
        return 0

    gate_load.wait()
    gain_load.wait()
    lax.fori_loop(0, NB, gating, 0)

    all_of(prefix_in.at[0:N_CTX - 1], scan_sem.at[3])

    ones = jnp.ones((8, HD), F32)

    def ssq_copy(there, slot):
        return pltpu.make_async_remote_copy(
            src_ref=ssq_out.at[there], dst_ref=ssq_in.at[slot],
            send_sem=scan_sem.at[4], recv_sem=scan_sem.at[5],
            device_id={"head": there}, device_id_type=pl.DeviceIdType.MESH)

    def finish(rb):
        dc = dec_col[rb]
        bd = before_dec[rb]
        square = jnp.zeros((BLOCK, HD), F32)
        for h in range(LH):
            lanes = slice(h * HD, (h + 1) * HD)
            carried = jnp.concatenate([prefix_in[2 * h], prefix_in[2 * h + 1]], axis=0)
            start = (bd[h:h + 1] * carried.astype(F32) + local[rb, h // 2, h % 2]).astype(BF16)
            qb = q_v[ds(rb, BLOCK), lanes]
            inter = jnp.dot(qb, start, preferred_element_type=F32)
            attn = intra[rb, :, lanes] + dc[:, h:h + 1] * inter
            square = square + attn * attn
            hidden = (attn * gated[rb, :, lanes]).astype(BF16)
            hid[rb, ds(1 - core, HALF), lanes] = hidden[:HALF]
            hid[rb, ds(core, HALF), lanes] = hidden[HALF:]
        sums = lax.dot_general(ones, square, nt, precision=HI, preferred_element_type=F32)
        for s in range(2):
            there = rb * 2 + s
            ssq_out[there] = sums[:, s * HALF:(s + 1) * HALF]

            @pl.when(there != head)
            def _():
                ssq_copy(there, head).start()

            @pl.when(there == head)
            def _():
                ssq_in[head] = ssq_out[head]

    def core_copy(phase, lane, j):
        slot = phase * NC + lane * NH + j
        return pltpu.make_async_remote_copy(
            src_ref=core_out.at[slot], dst_ref=core_in.at[slot],
            send_sem=core_ssem, recv_sem=core_rsem.at[lane, (phase * NH + j) % 4],
            device_id={"head": partner}, device_id_type=pl.DeviceIdType.MESH)

    def far_copy(n, there):
        return pltpu.make_async_remote_copy(
            src_ref=z_out.at[0, n], dst_ref=far_in.at[n],
            send_sem=z_ssem, recv_sem=far_rsem.at[n // 2],
            device_id={"head": there}, device_id_type=pl.DeviceIdType.MESH)

    def near_copy(side, n, there, sem):
        return pltpu.make_async_remote_copy(
            src_ref=z_out.at[1 + side, n], dst_ref=near_in.at[side, n],
            send_sem=z_ssem, recv_sem=sem,
            device_id={"head": there}, device_id_type=pl.DeviceIdType.MESH)

    def product(phase, lane, j, rb, n):
        r = jnp.dot(hid[rb], w_v[n], preferred_element_type=F32)
        core_out[phase * NC + lane * NH + j] = r[:HALF].astype(BF16)
        core_copy(phase, lane, j).start()
        return r[HALF:]

    def summed(phase, lane, j):
        core_copy(phase, lane, j).wait_recv()
        return own[lane] + core_in[phase * NC + lane * NH + j].astype(F32)

    def fin0(lane, j):
        n = lane * NH + j
        z_out[0, n] = summed(0, lane, j).astype(BF16)
        far_copy(n, right if lane == 0 else left).start()

    def fin1(lane, j):
        n = (1 - lane) * NH + j
        z_out[1 + lane, n] = summed(1, lane, j).astype(BF16)
        near_copy(lane, n, right if lane == 0 else left, early_rsem.at[lane]).start()

    def fin2(lane, j):
        n = lane * NH + j
        s = summed(2, lane, j)

        @pl.when(j % 2 == 0)
        def _():
            all_of(far_in.at[pl.ds(n, 2)], far_rsem.at[n // 2])

        z_out[1 + lane, n] = (s + far_in[n].astype(F32)).astype(BF16)
        near_copy(lane, n, right if lane == 0 else left, late_rsem.at[lane, j]).start()

    def keep_total(n, value):
        intra[n // 4, ds(n // 2 % 2, HALF), ds(n % 2, CN)] = value

    def kept_total(n):
        return intra[n // 4, ds(n // 2 % 2, HALF), ds(n % 2, CN)]

    def fin3(lane, j):
        n = lane * NH + j
        keep_total(n, summed(3, lane, j))

    def step(phase, lane, j):
        n = (1 - lane) * NH + j if phase == 1 else lane * NH + j
        if phase == 0:
            rb = zo
        elif phase == 3:
            rb = z
        else:
            rb = zr if lane == 0 else zl
        return product(phase, lane, j, rb, n)

    fins = (fin0, fin1, fin2, fin3)
    pending = None
    for phase in range(4):
        if phase == 0:
            finish(zo)
            all_of(w_v, once_sem.at[4])
        elif phase == 1:
            finish(zr)
            finish(zl)
        elif phase == 3:
            finish(z)
        for lane in range(2):
            r = step(phase, lane, 0)
            if pending is not None:
                pending(lane, NH - 1)
            own[lane] = r

        def body(j, _, phase=phase):
            for lane in range(2):
                r = step(phase, lane, j)
                fins[phase](lane, j - 1)
                own[lane] = r
            return 0

        lax.fori_loop(1, NH, body, 0)
        pending = fins[phase]
    for lane in range(2):
        pending(lane, NH - 1)

    all_of(ssq_in.at[0:N_HEAD - 1], scan_sem.at[5])
    squares = jnp.sum(ssq_in[...], axis=0)
    scale_row = lax.rsqrt(squares[0:1, :] * (1.0 / (HEADS * HD)) + EPS)
    scale = jnp.sum(
        jnp.where(r2 == c2, jnp.broadcast_to(scale_row, (HALF, HALF)), 0.0), axis=1, keepdims=True)

    all_of(near_in.at[0, NH:NC], early_rsem.at[0])
    all_of(near_in.at[1, 0:NH], early_rsem.at[1])

    def result(j, _):
        for lane in range(2):
            n = lane * NH + j
            near_copy(lane, n, right, late_rsem.at[lane, j]).wait_recv()
            s = kept_total(n) + near_in[0, n].astype(F32) + near_in[1, n].astype(F32)
            out_ref[:, ds(n, CN)] = (s * scale).astype(BF16)
        return 0

    lax.fori_loop(0, NH, result, 0)

    all_of(scan_out.at[0:N_CTX - 1], scan_sem.at[0])
    all_of(prefix_out.at[0:N_CTX - 1], scan_sem.at[2])
    all_of(ssq_out.at[0:N_HEAD - 1], scan_sem.at[4])
    all_of(core_out, core_ssem)
    all_of(z_out, z_ssem)


def shards(queries, keys, values, gate_logits, log_decay, norm_gain_vector, out_weight):
    any_spec = pl.BlockSpec(memory_space=pl.ANY)
    vmem = pl.BlockSpec(memory_space=pltpu.VMEM)
    dma = pltpu.SemaphoreType.DMA
    return pl.pallas_call(
        kernel,
        out_shape=pltpu.VMEM((ROWS // N_HEAD, D), BF16),
        in_specs=[any_spec] * 7,
        out_specs=vmem,
        scratch_shapes=[
            pltpu.VMEM((LH, ROWS), F32),
            pltpu.VMEM((1, WIDTH), F32),
            pltpu.VMEM((ROWS, WIDTH), BF16),
            pltpu.VMEM((ROWS, WIDTH), BF16),
            pltpu.VMEM((ROWS, WIDTH), BF16),
            pltpu.VMEM((ROWS, WIDTH), BF16),
            pltpu.VMEM((NC, WIDTH, CN), BF16),
            pltpu.VMEM((NB, BLOCK, WIDTH), BF16),
            pltpu.VMEM((NB, BLOCK, WIDTH), F32),
            pltpu.VMEM((NB, BLOCK, WIDTH), F32),
            pltpu.VMEM((NB, 4, 2, HD, HD), F32),
            pltpu.VMEM((NB, LH, BLOCK), F32),
            pltpu.VMEM((NB, BLOCK, LH), F32),
            pltpu.VMEM((NB, BLOCK, LH), F32),
            pltpu.VMEM((NB, LH, HD), F32),
            pltpu.VMEM((NB, 4, 2, BLOCK), F32),
            pltpu.VMEM((NB, 4, 2, HD), F32),
            pltpu.VMEM((4, 2, 16, HD), BF16),
            pltpu.VMEM((N_CTX, MSG, HD), BF16),
            pltpu.VMEM((N_CTX, MSG, HD), BF16),
            pltpu.VMEM((N_CTX, SL, HD), BF16),
            pltpu.VMEM((N_CTX, SL, HD), BF16),
            pltpu.VMEM((N_HEAD, 8, HALF), F32),
            pltpu.VMEM((N_HEAD, 8, HALF), F32),
            pltpu.VMEM((4 * NC, HALF, CN), BF16),
            pltpu.VMEM((4 * NC, HALF, CN), BF16),
            pltpu.VMEM((2, HALF, CN), F32),
            pltpu.VMEM((3, NC, HALF, CN), BF16),
            pltpu.VMEM((NC, HALF, CN), BF16),
            pltpu.VMEM((2, NC, HALF, CN), BF16),
            dma((2, NB)), dma((5,)), dma((6,)),
            dma, dma((2, 4)),
            dma, dma((NC // 2,)), dma((2,)), dma((2, NH)),
        ],
        compiler_params=pltpu.CompilerParams(
            collective_id=0, has_side_effects=True, vmem_limit_bytes=60 * 1024 * 1024),
        cost_estimate=pl.CostEstimate(
            flops=15_000_000_000, bytes_accessed=23_000_000, transcendentals=4_000_000),
        name="attention",
    )(queries, keys, values, gate_logits, log_decay, norm_gain_vector.reshape(1, WIDTH), out_weight)


def solution(mesh):
    in_specs = (
        P("ctx", "head"),
        P("ctx", "head"),
        P("ctx", "head"),
        P("ctx", "head"),
        P("head", "ctx"),
        P("head"),
        P("head", None),
    )
    out_specs = P(("ctx", "head"), None)
    return jax.shard_map(shards, mesh=mesh, in_specs=in_specs, out_specs=out_specs, check_vma=False)
```

```python
import functools

import jax
import jax.numpy as jnp
from jax import lax
from jax.experimental import pallas as pl
from jax.experimental.pallas import tpu as pltpu
from jax.sharding import PartitionSpec as P

HEADS = 64
HD = 128
BLOCK = 256
EPS = 1e-06

N_CTX = 16
N_HEAD = 8
ROWS = 1024
WIDTH = 1024
D = 6144
LH = 8
NB = 4
HALF = 128
PAIR = 2 * HD
CN = 512
NC = D // CN
NH = NC // 2
SL = LH * HD // N_CTX
MSG = SL + 16

F32 = jnp.float32
BF16 = jnp.bfloat16
HI = lax.Precision.HIGHEST


def ds(start, size):
    return pl.ds(pl.multiple_of(start * size, size), size)


def kernel(
    q_hbm, k_hbm, v_hbm, gate_hbm, decay_hbm, gain_hbm, w_hbm, out_ref,
    decay_ref, gain_ref,
    q_v, k_v, v_v, gate_v, w_v, hid, intra, gated, local,
    cum_row, cum_col, before_dec, factor, keep_dec, parts,
    scan_out, scan_in, prefix_out, prefix_in, ssq_out, ssq_in,
    core_out, core_in, own, z_out, far_in, near_in,
    load_sem, once_sem, scan_sem, scan_rsem, carried_sem, core_ssem, core_rsem, z_ssem, far_rsem, early_rsem, late_rsem,
):
    ctx = lax.axis_index("ctx")
    head = lax.axis_index("head")
    z = head // 2
    core = head % 2
    partner = z * 2 + (1 - core)
    zr = (z + 1) % 4
    zl = (z + 3) % 4
    zo = (z + 2) % 4
    right = zr * 2 + core
    left = zl * 2 + core

    def load(src, dst, sem):
        return pltpu.make_async_copy(src, dst, sem)

    def block_load(i, src, dst, b):
        return load(src.at[ds(b, BLOCK)], dst.at[ds(b, BLOCK)], load_sem.at[i, b])

    def w_load(n):
        return load(w_hbm.at[:, ds(n, CN)], w_v.at[n], once_sem.at[4])

    q_load = load(q_hbm, q_v, once_sem.at[0])
    gate_load = load(gate_hbm, gate_v, once_sem.at[1])
    decay_load = load(decay_hbm, decay_ref, once_sem.at[2])
    gain_load = load(gain_hbm, gain_ref, once_sem.at[3])
    decay_load.start()

    def all_of(ref, sem):
        load(ref, ref, sem).wait()

    ctx_y = ctx // 4
    ctx_x = ctx % 4
    far_first = (2, 1, 3, 0)
    pairs = [(ctx_y + off) % 4 for off in far_first]
    barrier = pltpu.get_barrier_semaphore()
    for dy in far_first:
        for dx in far_first:
            if dy or dx:
                pl.semaphore_signal(
                    barrier, inc=1, device_id={"ctx": (ctx_y + dy) % 4 * 4 + (ctx_x + dx) % 4},
                    device_id_type=pl.DeviceIdType.MESH)

    for b in range(NB):
        block_load(0, k_hbm, k_v, b).start()
        block_load(1, v_hbm, v_v, b).start()

    def greet_head(d, _):
        pl.semaphore_signal(barrier, inc=1, device_id={"head": (head + d) % N_HEAD},
                            device_id_type=pl.DeviceIdType.MESH)
        return 0

    lax.fori_loop(1, N_HEAD, greet_head, 0)

    ri = lax.broadcasted_iota(jnp.int32, (BLOCK, BLOCK), 0)
    ci = lax.broadcasted_iota(jnp.int32, (BLOCK, BLOCK), 1)
    lower = (ri >= ci).astype(F32)
    eye = (ri == ci).astype(BF16)
    nt = (((1,), (1,)), ((), ()))
    before = jnp.zeros((LH, 1), F32)
    tile = lax.broadcasted_iota(jnp.int32, (16, HD), 0)
    decay_load.wait()
    blocks = jnp.concatenate([decay_ref[:, b * BLOCK:(b + 1) * BLOCK] for b in range(NB)], axis=0)
    high = blocks.astype(BF16).astype(F32)
    middle = (blocks - high).astype(BF16).astype(F32)
    thirds = jnp.concatenate([high, middle, blocks - high - middle], axis=0).astype(BF16)
    sums = lax.dot_general(thirds, lower.astype(BF16), nt, preferred_element_type=F32)
    all_rows = sums[:NB * LH] + (sums[NB * LH:2 * NB * LH] + sums[2 * NB * LH:])
    for b in range(NB):
        row = all_rows[b * LH:(b + 1) * LH]
        cum_row[b] = row
        last = row[:, BLOCK - 1:BLOCK]
        fac = jnp.exp(row - last)
        kept = jnp.broadcast_to(jnp.exp(-last), (LH, HD))
        entry = jnp.broadcast_to(jnp.exp(-before), (LH, HD))
        before = before + last
        for p in range(4):
            factor[b, p] = fac[2 * p:2 * p + 2]
            keep_dec[b, p] = kept[2 * p:2 * p + 2]
            before_dec[b, p] = entry[2 * p:2 * p + 2]
    shard_dec = jnp.broadcast_to(jnp.exp(-before), (LH, HD))
    for h in range(LH):
        a = jnp.broadcast_to(shard_dec[h:h + 1], (16, HD))
        hi = a.astype(BF16).astype(F32)
        mid = (a - hi).astype(BF16).astype(F32)
        low = a - hi - mid
        part = jnp.where(tile == 0, hi, jnp.where(tile == 1, mid, jnp.where(tile == 2, low, 0.0)))
        parts[h // 2, h % 2] = part.astype(BF16)

    def scan_copy(there, slot):
        return pltpu.make_async_remote_copy(
            src_ref=scan_out.at[there], dst_ref=scan_in.at[slot],
            send_sem=scan_sem.at[0], recv_sem=scan_rsem.at[ctx_y],
            device_id={"ctx": there}, device_id_type=pl.DeviceIdType.MESH)

    def prefix_copy(there, slot):
        return pltpu.make_async_remote_copy(
            src_ref=prefix_out.at[there], dst_ref=prefix_in.at[slot],
            send_sem=scan_sem.at[2], recv_sem=carried_sem.at[ctx_y],
            device_id={"ctx": there}, device_id_type=pl.DeviceIdType.MESH)

    def added(b, p):
        rows = slice(b * BLOCK, (b + 1) * BLOCK)
        lanes = ds(p, PAIR)
        flipped = lax.dot_general(eye, k_v[rows, lanes], nt, preferred_element_type=F32)
        vb = v_v[rows, lanes]
        new = []
        for s in range(2):
            kd = (flipped[s * HD:(s + 1) * HD] * factor[b, p, s:s + 1, :]).astype(BF16)
            new.append(jnp.dot(kd, vb[:, s * HD:(s + 1) * HD], preferred_element_type=F32))
        return new

    for b in range(NB - 1):
        block_load(0, k_hbm, k_v, b).wait()
        block_load(1, v_hbm, v_v, b).wait()
        for p in range(4):
            for s, new in enumerate(added(b, p)):
                if b == 0:
                    local[0, p, s] = jnp.zeros((HD, HD), F32)
                else:
                    new = new + keep_dec[b, p, s:s + 1, :] * local[b, p, s]
                local[b + 1, p, s] = new

    block_load(0, k_hbm, k_v, NB - 1).wait()
    block_load(1, v_hbm, v_v, NB - 1).wait()
    q_load.start()

    for i, p in enumerate(pairs):
        for s, new in enumerate(added(NB - 1, p)):
            state = new + keep_dec[NB - 1, p, s:s + 1, :] * local[NB - 1, p, s]
            for t in range(2):
                scan_out[4 * p + 2 * s + t, 0:SL] = state[t * SL:(t + 1) * SL].astype(BF16)
                scan_out[4 * p + 2 * s + t, SL:MSG] = parts[p, s]
        if i == 0:
            pl.semaphore_wait(barrier, N_CTX - 1 + N_HEAD - 1)
        for off in far_first:
            there = 4 * p + (ctx_x + off) % 4
            if far_first[i] == 0 and off == 0:
                scan_in[ctx] = scan_out[ctx]
            else:
                scan_copy(there, ctx).start()

    all_cols = lax.dot_general(lower, blocks, nt, precision=HI, preferred_element_type=F32)
    for b in range(NB):
        cum_col[b] = all_cols[:, b * LH:(b + 1) * LH]

    r2 = lax.broadcasted_iota(jnp.int32, (HALF, HALF), 0)
    c2 = lax.broadcasted_iota(jnp.int32, (HALF, HALF), 1)
    keep = r2 >= c2

    def inside(b):
        rows = cum_row[b]
        cols = cum_col[b]
        for h in range(LH):
            lanes = slice(h * HD, (h + 1) * HD)
            qb = q_v[ds(b, BLOCK), lanes]
            kb = k_v[ds(b, BLOCK), lanes]
            vb = v_v[ds(b, BLOCK), lanes]
            scores = lax.dot_general(qb, kb, nt, preferred_element_type=F32)
            cr = rows[h:h + 1, :]
            cc = jnp.broadcast_to(cols[:, h:h + 1], (BLOCK, HALF))
            top = jnp.where(keep, scores[:HALF, :HALF] * jnp.exp(cr[:, :HALF] - cc[:HALF]), 0.0)
            bl = scores[HALF:, :HALF] * jnp.exp(cr[:, :HALF] - cc[HALF:])
            br = jnp.where(keep, scores[HALF:, HALF:] * jnp.exp(cr[:, HALF:] - cc[HALF:]), 0.0)
            a0 = jnp.dot(top.astype(BF16), vb[:HALF], preferred_element_type=F32)
            bottom = jnp.concatenate([bl.astype(BF16), br.astype(BF16)], axis=1)
            a1 = jnp.dot(bottom, vb, preferred_element_type=F32)
            intra[b, :HALF, lanes] = a0
            intra[b, HALF:, lanes] = a1
            q_v[ds(b, BLOCK), lanes] = (qb.astype(F32) * jnp.exp(-cc)).astype(BF16)

    def prefixes(y, state):
        for own_row in (False, True):
            @pl.when((ctx_y == y) == own_row)
            def _():
                all_of(scan_in.at[0:3 if own_row else 4], scan_rsem.at[y])

        for s in range(4 * y, 4 * y + 4):
            if s < N_CTX - 1:
                dec = jnp.sum(scan_in[s, SL:MSG].astype(F32), axis=0, keepdims=True)
                state = dec * state + scan_in[s, 0:SL].astype(F32)
                prefix_out[s + 1] = state.astype(BF16)
        for s in range(4 * y + 1, min(4 * y + 5, N_CTX)):
            @pl.when(s != ctx)
            def _():
                prefix_copy(s, ctx).start()
        return state

    q_load.wait()
    gate_load.start()
    gain_load.start()
    for j in range(NH):
        w_load(j).start()
        w_load(NH + j).start()
    state = jnp.zeros((SL, HD), F32)
    for y in range(4):
        state = prefixes(y, state)

    @pl.when(ctx == 0)
    def _():
        prefix_in[...] = jnp.zeros_like(prefix_in)

    @pl.when(ctx != 0)
    def _():
        prefix_in[ctx] = prefix_out[ctx]

    def gating(b):
        for h in range(LH):
            lanes = slice(h * HD, (h + 1) * HD)
            gl = gate_v[ds(b, BLOCK), lanes].astype(F32)
            gated[b, :, lanes] = jax.nn.sigmoid(gl) * gain_ref[:, lanes]

    gate_load.wait()
    gain_load.wait()
    inside(zo)
    gating(zo)

    ones = jnp.ones((8, HD), F32)

    def ssq_copy(there, slot):
        return pltpu.make_async_remote_copy(
            src_ref=ssq_out.at[there], dst_ref=ssq_in.at[slot],
            send_sem=scan_sem.at[3], recv_sem=scan_sem.at[4],
            device_id={"head": there}, device_id_type=pl.DeviceIdType.MESH)

    def finish(rb, first=False):
        square = jnp.zeros((BLOCK, HD), F32)
        for i, p in enumerate((ctx_y + off) % 4 for off in (0, 1, 3, 2)):
            if first:
                @pl.when(ctx != 0)
                def _(i=i, p=p):
                    all_of(prefix_in.at[0:4 - (1 if i == 0 else 0)], carried_sem.at[p])

            for s in range(2):
                lanes = ds(2 * p + s, HD)
                carried = jnp.concatenate([prefix_in[4 * p + 2 * s], prefix_in[4 * p + 2 * s + 1]], axis=0)
                start = before_dec[rb, p, s:s + 1, :] * carried.astype(F32) + local[rb, p, s]
                inter = jnp.dot(q_v[ds(rb, BLOCK), lanes], start.astype(BF16), preferred_element_type=F32)
                attn = intra[rb, :, lanes] + inter
                square = square + attn * attn
                hidden = (attn * gated[rb, :, lanes]).astype(BF16)
                hid[rb, ds(1 - core, HALF), lanes] = hidden[:HALF]
                hid[rb, ds(core, HALF), lanes] = hidden[HALF:]
        return square

    def send_squares(rb, square):
        sums = lax.dot_general(ones, square, nt, precision=HI, preferred_element_type=F32)
        for s in range(2):
            there = rb * 2 + s
            ssq_out[there] = sums[:, s * HALF:(s + 1) * HALF]

            @pl.when(there != head)
            def _():
                ssq_copy(there, head).start()

            @pl.when(there == head)
            def _():
                ssq_in[head] = ssq_out[head]

    def core_copy(phase, lane, j):
        slot = phase * NC + lane * NH + j
        return pltpu.make_async_remote_copy(
            src_ref=core_out.at[slot], dst_ref=core_in.at[slot],
            send_sem=core_ssem, recv_sem=core_rsem.at[lane, (phase * NH + j) % 4],
            device_id={"head": partner}, device_id_type=pl.DeviceIdType.MESH)

    def far_copy(n, there):
        return pltpu.make_async_remote_copy(
            src_ref=z_out.at[0, n], dst_ref=far_in.at[n],
            send_sem=z_ssem, recv_sem=far_rsem.at[n // 2],
            device_id={"head": there}, device_id_type=pl.DeviceIdType.MESH)

    def near_copy(side, n, there, sem):
        return pltpu.make_async_remote_copy(
            src_ref=z_out.at[1 + side, n], dst_ref=near_in.at[side, n],
            send_sem=z_ssem, recv_sem=sem,
            device_id={"head": there}, device_id_type=pl.DeviceIdType.MESH)

    def product(phase, lane, j, rb, n):
        r = jnp.dot(hid[rb], w_v[n], preferred_element_type=F32)
        core_out[phase * NC + lane * NH + j] = r[:HALF].astype(BF16)
        core_copy(phase, lane, j).start()
        return r[HALF:]

    def summed(phase, lane, j):
        core_copy(phase, lane, j).wait_recv()
        return own[lane] + core_in[phase * NC + lane * NH + j].astype(F32)

    def fin0(lane, j):
        n = lane * NH + j
        z_out[0, n] = summed(0, lane, j).astype(BF16)
        far_copy(n, right if lane == 0 else left).start()

    def fin1(lane, j):
        n = (1 - lane) * NH + j
        z_out[1 + lane, n] = summed(1, lane, j).astype(BF16)
        near_copy(lane, n, right if lane == 0 else left, early_rsem.at[lane]).start()

    def fin2(lane, j):
        n = lane * NH + j
        s = summed(2, lane, j)

        @pl.when(j % 2 == 0)
        def _():
            all_of(far_in.at[pl.ds(n, 2)], far_rsem.at[n // 2])

        z_out[1 + lane, n] = (s + far_in[n].astype(F32)).astype(BF16)
        near_copy(lane, n, right if lane == 0 else left, late_rsem.at[lane, j]).start()

    def keep_total(n, value):
        intra[n // 4, ds(n // 2 % 2, HALF), ds(n % 2, CN)] = value

    def kept_total(n):
        return intra[n // 4, ds(n // 2 % 2, HALF), ds(n % 2, CN)]

    def fin3(lane, j):
        n = lane * NH + j
        keep_total(n, summed(3, lane, j))

    def step(phase, lane, j):
        n = (1 - lane) * NH + j if phase == 1 else lane * NH + j
        if phase == 0:
            rb = zo
        elif phase == 3:
            rb = z
        else:
            rb = zr if lane == 0 else zl
        return product(phase, lane, j, rb, n)

    fins = (fin0, fin1, fin2, fin3)
    pending = None
    for phase in range(4):
        if phase == 0:
            square = finish(zo, first=True)
            all_of(w_v, once_sem.at[4])
        elif phase == 1:
            send_squares(zo, square)
            for rb in (zr, zl):
                inside(rb)
                gating(rb)
                send_squares(rb, finish(rb))
        elif phase == 3:
            inside(z)
            gating(z)
            send_squares(z, finish(z))
        for lane in range(2):
            r = step(phase, lane, 0)
            if pending is not None:
                pending(lane, NH - 1)
            own[lane] = r

        def body(j, _, phase=phase):
            for lane in range(2):
                r = step(phase, lane, j)
                fins[phase](lane, j - 1)
                own[lane] = r
            return 0

        lax.fori_loop(1, NH, body, 0)
        pending = fins[phase]
    for lane in range(2):
        pending(lane, NH - 1)

    all_of(ssq_in.at[0:N_HEAD - 1], scan_sem.at[4])
    squares = jnp.sum(ssq_in[...], axis=0)
    scale_row = lax.rsqrt(squares[0:1, :] * (1.0 / (HEADS * HD)) + EPS)
    scale = jnp.sum(
        jnp.where(r2 == c2, jnp.broadcast_to(scale_row, (HALF, HALF)), 0.0), axis=1, keepdims=True)

    all_of(near_in.at[0, NH:NC], early_rsem.at[0])
    all_of(near_in.at[1, 0:NH], early_rsem.at[1])

    def result(j, _):
        for lane in range(2):
            n = lane * NH + j
            near_copy(lane, n, right, late_rsem.at[lane, j]).wait_recv()
            s = kept_total(n) + near_in[0, n].astype(F32) + near_in[1, n].astype(F32)
            out_ref[:, ds(n, CN)] = (s * scale).astype(BF16)
        return 0

    lax.fori_loop(0, NH, result, 0)

    all_of(scan_out.at[0:N_CTX - 1], scan_sem.at[0])
    all_of(prefix_out.at[0:N_CTX - 2], scan_sem.at[2])

    @pl.when(ctx == 0)
    def _():
        all_of(prefix_out.at[0:1], scan_sem.at[2])

    all_of(ssq_out.at[0:N_HEAD - 1], scan_sem.at[3])
    all_of(core_out, core_ssem)
    all_of(z_out, z_ssem)


def shards(queries, keys, values, gate_logits, log_decay, norm_gain_vector, out_weight):
    any_spec = pl.BlockSpec(memory_space=pl.ANY)
    vmem = pl.BlockSpec(memory_space=pltpu.VMEM)
    dma = pltpu.SemaphoreType.DMA
    return pl.pallas_call(
        kernel,
        out_shape=pltpu.VMEM((ROWS // N_HEAD, D), BF16),
        in_specs=[any_spec] * 7,
        out_specs=vmem,
        scratch_shapes=[
            pltpu.VMEM((LH, ROWS), F32),
            pltpu.VMEM((1, WIDTH), F32),
            pltpu.VMEM((ROWS, WIDTH), BF16),
            pltpu.VMEM((ROWS, WIDTH), BF16),
            pltpu.VMEM((ROWS, WIDTH), BF16),
            pltpu.VMEM((ROWS, WIDTH), BF16),
            pltpu.VMEM((NC, WIDTH, CN), BF16),
            pltpu.VMEM((NB, BLOCK, WIDTH), BF16),
            pltpu.VMEM((NB, BLOCK, WIDTH), F32),
            pltpu.VMEM((NB, BLOCK, WIDTH), F32),
            pltpu.VMEM((NB, 4, 2, HD, HD), F32),
            pltpu.VMEM((NB, LH, BLOCK), F32),
            pltpu.VMEM((NB, BLOCK, LH), F32),
            pltpu.VMEM((NB, 4, 2, HD), F32),
            pltpu.VMEM((NB, 4, 2, BLOCK), F32),
            pltpu.VMEM((NB, 4, 2, HD), F32),
            pltpu.VMEM((4, 2, 16, HD), BF16),
            pltpu.VMEM((N_CTX, MSG, HD), BF16),
            pltpu.VMEM((N_CTX, MSG, HD), BF16),
            pltpu.VMEM((N_CTX, SL, HD), BF16),
            pltpu.VMEM((N_CTX, SL, HD), BF16),
            pltpu.VMEM((N_HEAD, 8, HALF), F32),
            pltpu.VMEM((N_HEAD, 8, HALF), F32),
            pltpu.VMEM((4 * NC, HALF, CN), BF16),
            pltpu.VMEM((4 * NC, HALF, CN), BF16),
            pltpu.VMEM((2, HALF, CN), F32),
            pltpu.VMEM((3, NC, HALF, CN), BF16),
            pltpu.VMEM((NC, HALF, CN), BF16),
            pltpu.VMEM((2, NC, HALF, CN), BF16),
            dma((2, NB)), dma((5,)), dma((5,)), dma((4,)), dma((4,)),
            dma, dma((2, 4)),
            dma, dma((NC // 2,)), dma((2,)), dma((2, NH)),
        ],
        compiler_params=pltpu.CompilerParams(
            collective_id=0, has_side_effects=True, vmem_limit_bytes=60 * 1024 * 1024),
        cost_estimate=pl.CostEstimate(
            flops=15_000_000_000, bytes_accessed=23_000_000, transcendentals=4_000_000),
        name="attention",
    )(queries, keys, values, gate_logits, log_decay, norm_gain_vector.reshape(1, WIDTH), out_weight)


def solution(mesh):
    in_specs = (
        P("ctx", "head"),
        P("ctx", "head"),
        P("ctx", "head"),
        P("ctx", "head"),
        P("head", "ctx"),
        P("head"),
        P("head", None),
    )
    out_specs = P(("ctx", "head"), None)
    return jax.shard_map(shards, mesh=mesh, in_specs=in_specs, out_specs=out_specs, check_vma=False)
```

```python
import functools

import jax
import jax.numpy as jnp
from jax import lax
from jax.experimental import pallas as pl
from jax.experimental.pallas import tpu as pltpu
from jax.sharding import PartitionSpec as P

HEADS = 64
HD = 128
BLOCK = 256
EPS = 1e-06

N_CTX = 16
N_HEAD = 8
ROWS = 1024
WIDTH = 1024
D = 6144
LH = 8
NB = 4
HALF = 128
PAIR = 2 * HD
CN = 512
NC = D // CN
NH = NC // 2
SL = LH * HD // N_CTX
MSG = SL + 16

F32 = jnp.float32
BF16 = jnp.bfloat16
HI = lax.Precision.HIGHEST


def ds(start, size):
    return pl.ds(pl.multiple_of(start * size, size), size)


def kernel(
    q_hbm, k_hbm, v_hbm, gate_hbm, decay_hbm, gain_hbm, w_hbm, out_ref,
    decay_ref, gain_ref,
    q_v, k_v, v_v, gate_v, w_v, hid, intra, gated, local,
    cum_row, cum_col, before_dec, factor, keep_dec, parts,
    scan_out, scan_in, prefix_out, prefix_in, ssq_out, ssq_in,
    core_out, core_in, own, z_out, far_in, near_in,
    load_sem, once_sem, scan_sem, scan_rsem, carried_sem, core_ssem, core_rsem, z_ssem, far_rsem, early_rsem, late_rsem,
):
    ctx = lax.axis_index("ctx")
    head = lax.axis_index("head")
    z = head // 2
    core = head % 2
    partner = z * 2 + (1 - core)
    zr = (z + 1) % 4
    zl = (z + 3) % 4
    zo = (z + 2) % 4
    right = zr * 2 + core
    left = zl * 2 + core

    def load(src, dst, sem):
        return pltpu.make_async_copy(src, dst, sem)

    def block_load(i, src, dst, b):
        return load(src.at[ds(b, BLOCK)], dst.at[ds(b, BLOCK)], load_sem.at[i, b])

    def w_load(n):
        return load(w_hbm.at[:, ds(n, CN)], w_v.at[n], once_sem.at[4])

    q_load = load(q_hbm, q_v, once_sem.at[0])
    gate_load = load(gate_hbm, gate_v, once_sem.at[1])
    decay_load = load(decay_hbm, decay_ref, once_sem.at[2])
    gain_load = load(gain_hbm, gain_ref, once_sem.at[3])
    decay_load.start()

    def all_of(ref, sem):
        load(ref, ref, sem).wait()

    ctx_y = ctx // 4
    ctx_x = ctx % 4
    far_first = (2, 1, 3, 0)
    pairs = [(ctx_y + off) % 4 for off in far_first]
    barrier = pltpu.get_barrier_semaphore()
    for dy in far_first:
        for dx in far_first:
            if dy or dx:
                pl.semaphore_signal(
                    barrier, inc=1, device_id={"ctx": (ctx_y + dy) % 4 * 4 + (ctx_x + dx) % 4},
                    device_id_type=pl.DeviceIdType.MESH)

    for b in range(NB):
        block_load(0, k_hbm, k_v, b).start()
        block_load(1, v_hbm, v_v, b).start()

    def greet_head(d, _):
        pl.semaphore_signal(barrier, inc=1, device_id={"head": (head + d) % N_HEAD},
                            device_id_type=pl.DeviceIdType.MESH)
        return 0

    lax.fori_loop(1, N_HEAD, greet_head, 0)

    ri = lax.broadcasted_iota(jnp.int32, (BLOCK, BLOCK), 0)
    ci = lax.broadcasted_iota(jnp.int32, (BLOCK, BLOCK), 1)
    lower = (ri >= ci).astype(F32)
    eye = (ri == ci).astype(BF16)
    nt = (((1,), (1,)), ((), ()))
    before = jnp.zeros((LH, 1), F32)
    tile = lax.broadcasted_iota(jnp.int32, (16, HD), 0)
    decay_load.wait()
    blocks = jnp.concatenate([decay_ref[:, b * BLOCK:(b + 1) * BLOCK] for b in range(NB)], axis=0)
    high = blocks.astype(BF16).astype(F32)
    middle = (blocks - high).astype(BF16).astype(F32)
    thirds = jnp.concatenate([high, middle, blocks - high - middle], axis=0).astype(BF16)
    sums = lax.dot_general(thirds, lower.astype(BF16), nt, preferred_element_type=F32)
    all_rows = sums[:NB * LH] + (sums[NB * LH:2 * NB * LH] + sums[2 * NB * LH:])
    for b in range(NB):
        row = all_rows[b * LH:(b + 1) * LH]
        cum_row[b] = row
        last = row[:, BLOCK - 1:BLOCK]
        fac = jnp.exp(row - last)
        kept = jnp.broadcast_to(jnp.exp(-last), (LH, HD))
        entry = jnp.broadcast_to(jnp.exp(-before), (LH, HD))
        before = before + last
        for p in range(4):
            factor[b, p] = fac[2 * p:2 * p + 2]
            keep_dec[b, p] = kept[2 * p:2 * p + 2]
            before_dec[b, p] = entry[2 * p:2 * p + 2]
    shard_dec = jnp.broadcast_to(jnp.exp(-before), (LH, HD))
    for h in range(LH):
        a = jnp.broadcast_to(shard_dec[h:h + 1], (16, HD))
        hi = a.astype(BF16).astype(F32)
        mid = (a - hi).astype(BF16).astype(F32)
        low = a - hi - mid
        part = jnp.where(tile == 0, hi, jnp.where(tile == 1, mid, jnp.where(tile == 2, low, 0.0)))
        parts[h // 2, h % 2] = part.astype(BF16)

    def scan_copy(there, slot):
        return pltpu.make_async_remote_copy(
            src_ref=scan_out.at[there], dst_ref=scan_in.at[slot],
            send_sem=scan_sem.at[0], recv_sem=scan_rsem.at[ctx_y],
            device_id={"ctx": there}, device_id_type=pl.DeviceIdType.MESH)

    def prefix_copy(there, slot):
        return pltpu.make_async_remote_copy(
            src_ref=prefix_out.at[there], dst_ref=prefix_in.at[slot],
            send_sem=scan_sem.at[2], recv_sem=carried_sem.at[ctx_y],
            device_id={"ctx": there}, device_id_type=pl.DeviceIdType.MESH)

    def added(b, p):
        rows = slice(b * BLOCK, (b + 1) * BLOCK)
        lanes = ds(p, PAIR)
        flipped = lax.dot_general(eye, k_v[rows, lanes], nt, preferred_element_type=F32)
        vb = v_v[rows, lanes]
        new = []
        for s in range(2):
            kd = (flipped[s * HD:(s + 1) * HD] * factor[b, p, s:s + 1, :]).astype(BF16)
            new.append(jnp.dot(kd, vb[:, s * HD:(s + 1) * HD], preferred_element_type=F32))
        return new

    for b in range(NB - 1):
        block_load(0, k_hbm, k_v, b).wait()
        block_load(1, v_hbm, v_v, b).wait()
        for p in range(4):
            for s, new in enumerate(added(b, p)):
                if b == 0:
                    local[0, p, s] = jnp.zeros((HD, HD), F32)
                else:
                    new = new + keep_dec[b, p, s:s + 1, :] * local[b, p, s]
                local[b + 1, p, s] = new

    block_load(0, k_hbm, k_v, NB - 1).wait()
    block_load(1, v_hbm, v_v, NB - 1).wait()
    q_load.start()

    for i, p in enumerate(pairs):
        for s, new in enumerate(added(NB - 1, p)):
            state = new + keep_dec[NB - 1, p, s:s + 1, :] * local[NB - 1, p, s]
            for t in range(2):
                scan_out[4 * p + 2 * s + t, 0:SL] = state[t * SL:(t + 1) * SL].astype(BF16)
                scan_out[4 * p + 2 * s + t, SL:MSG] = parts[p, s]
        if i == 0:
            for j in range(NH):
                w_load(j).start()
                w_load(NH + j).start()
            pl.semaphore_wait(barrier, N_CTX - 1 + N_HEAD - 1)
        for off in far_first:
            there = 4 * p + (ctx_x + off) % 4
            if far_first[i] == 0 and off == 0:
                scan_in[ctx] = scan_out[ctx]
            else:
                scan_copy(there, ctx).start()

    all_cols = lax.dot_general(lower, blocks, nt, precision=HI, preferred_element_type=F32)
    for b in range(NB):
        cum_col[b] = all_cols[:, b * LH:(b + 1) * LH]

    r2 = lax.broadcasted_iota(jnp.int32, (HALF, HALF), 0)
    c2 = lax.broadcasted_iota(jnp.int32, (HALF, HALF), 1)
    keep = r2 >= c2

    def inside(b):
        rows = cum_row[b]
        cols = cum_col[b]
        for h in range(LH):
            lanes = slice(h * HD, (h + 1) * HD)
            qb = q_v[ds(b, BLOCK), lanes]
            kb = k_v[ds(b, BLOCK), lanes]
            vb = v_v[ds(b, BLOCK), lanes]
            scores = lax.dot_general(qb, kb, nt, preferred_element_type=F32)
            cr = rows[h:h + 1, :]
            cc = jnp.broadcast_to(cols[:, h:h + 1], (BLOCK, HALF))
            top = jnp.where(keep, scores[:HALF, :HALF] * jnp.exp(cr[:, :HALF] - cc[:HALF]), 0.0)
            bl = scores[HALF:, :HALF] * jnp.exp(cr[:, :HALF] - cc[HALF:])
            br = jnp.where(keep, scores[HALF:, HALF:] * jnp.exp(cr[:, HALF:] - cc[HALF:]), 0.0)
            a0 = jnp.dot(top.astype(BF16), vb[:HALF], preferred_element_type=F32)
            bottom = jnp.concatenate([bl.astype(BF16), br.astype(BF16)], axis=1)
            a1 = jnp.dot(bottom, vb, preferred_element_type=F32)
            intra[b, :HALF, lanes] = a0
            intra[b, HALF:, lanes] = a1
            q_v[ds(b, BLOCK), lanes] = (qb.astype(F32) * jnp.exp(-cc)).astype(BF16)

    def prefixes(y, state):
        for own_row in (False, True):
            @pl.when((ctx_y == y) == own_row)
            def _():
                all_of(scan_in.at[0:3 if own_row else 4], scan_rsem.at[y])

        for s in range(4 * y, 4 * y + 4):
            if s < N_CTX - 1:
                dec = jnp.sum(scan_in[s, SL:MSG].astype(F32), axis=0, keepdims=True)
                state = dec * state + scan_in[s, 0:SL].astype(F32)
                prefix_out[s + 1] = state.astype(BF16)
        for s in ([4 * y + 4] if y < 3 else []) + [4 * y + 1, 4 * y + 2, 4 * y + 3]:
            @pl.when(s != ctx)
            def _():
                prefix_copy(s, ctx).start()
        return state

    q_load.wait()
    gate_load.start()
    gain_load.start()
    state = jnp.zeros((SL, HD), F32)
    for y in range(4):
        state = prefixes(y, state)

    @pl.when(ctx == 0)
    def _():
        prefix_in[...] = jnp.zeros_like(prefix_in)

    @pl.when(ctx != 0)
    def _():
        prefix_in[ctx] = prefix_out[ctx]

    def gating(b):
        for h in range(LH):
            lanes = slice(h * HD, (h + 1) * HD)
            gl = gate_v[ds(b, BLOCK), lanes].astype(F32)
            gated[b, :, lanes] = jax.nn.sigmoid(gl) * gain_ref[:, lanes]

    gate_load.wait()
    gain_load.wait()
    inside(zo)
    gating(zo)

    ones = jnp.ones((8, HD), F32)

    def ssq_copy(there, slot):
        return pltpu.make_async_remote_copy(
            src_ref=ssq_out.at[there], dst_ref=ssq_in.at[slot],
            send_sem=scan_sem.at[3], recv_sem=scan_sem.at[4],
            device_id={"head": there}, device_id_type=pl.DeviceIdType.MESH)

    def finish(rb, first=False):
        square = jnp.zeros((BLOCK, HD), F32)
        for i, p in enumerate((ctx_y + off) % 4 for off in (0, 1, 3, 2)):
            if first:
                @pl.when(ctx != 0)
                def _(i=i, p=p):
                    all_of(prefix_in.at[0:4 - (1 if i == 0 else 0)], carried_sem.at[p])

            for s in range(2):
                lanes = ds(2 * p + s, HD)
                carried = jnp.concatenate([prefix_in[4 * p + 2 * s], prefix_in[4 * p + 2 * s + 1]], axis=0)
                start = before_dec[rb, p, s:s + 1, :] * carried.astype(F32) + local[rb, p, s]
                inter = jnp.dot(q_v[ds(rb, BLOCK), lanes], start.astype(BF16), preferred_element_type=F32)
                attn = intra[rb, :, lanes] + inter
                square = square + attn * attn
                hidden = (attn * gated[rb, :, lanes]).astype(BF16)
                hid[rb, ds(1 - core, HALF), lanes] = hidden[:HALF]
                hid[rb, ds(core, HALF), lanes] = hidden[HALF:]
        return square

    def send_squares(rb, square):
        sums = lax.dot_general(ones, square, nt, precision=HI, preferred_element_type=F32)
        for s in range(2):
            there = rb * 2 + s
            ssq_out[there] = sums[:, s * HALF:(s + 1) * HALF]

            @pl.when(there != head)
            def _():
                ssq_copy(there, head).start()

            @pl.when(there == head)
            def _():
                ssq_in[head] = ssq_out[head]

    def core_copy(phase, lane, j):
        slot = phase * NC + lane * NH + j
        return pltpu.make_async_remote_copy(
            src_ref=core_out.at[slot], dst_ref=core_in.at[slot],
            send_sem=core_ssem, recv_sem=core_rsem.at[lane, (phase * NH + j) % 4],
            device_id={"head": partner}, device_id_type=pl.DeviceIdType.MESH)

    def far_copy(n, there):
        return pltpu.make_async_remote_copy(
            src_ref=z_out.at[0, n], dst_ref=far_in.at[n],
            send_sem=z_ssem, recv_sem=far_rsem.at[n // 2],
            device_id={"head": there}, device_id_type=pl.DeviceIdType.MESH)

    def near_copy(side, n, there, sem):
        return pltpu.make_async_remote_copy(
            src_ref=z_out.at[1 + side, n], dst_ref=near_in.at[side, n],
            send_sem=z_ssem, recv_sem=sem,
            device_id={"head": there}, device_id_type=pl.DeviceIdType.MESH)

    def product(phase, lane, j, rb, n):
        r = jnp.dot(hid[rb], w_v[n], preferred_element_type=F32)
        core_out[phase * NC + lane * NH + j] = r[:HALF].astype(BF16)
        core_copy(phase, lane, j).start()
        return r[HALF:]

    def summed(phase, lane, j):
        core_copy(phase, lane, j).wait_recv()
        return own[lane] + core_in[phase * NC + lane * NH + j].astype(F32)

    def fin0(lane, j):
        n = lane * NH + j
        z_out[0, n] = summed(0, lane, j).astype(BF16)
        far_copy(n, right if lane == 0 else left).start()

    def fin1(lane, j):
        n = (1 - lane) * NH + j
        z_out[1 + lane, n] = summed(1, lane, j).astype(BF16)
        near_copy(lane, n, right if lane == 0 else left, early_rsem.at[lane]).start()

    def fin2(lane, j):
        n = lane * NH + j
        s = summed(2, lane, j)

        @pl.when(j % 2 == 0)
        def _():
            all_of(far_in.at[pl.ds(n, 2)], far_rsem.at[n // 2])

        z_out[1 + lane, n] = (s + far_in[n].astype(F32)).astype(BF16)
        near_copy(lane, n, right if lane == 0 else left, late_rsem.at[lane, j]).start()

    def keep_total(n, value):
        intra[n // 4, ds(n // 2 % 2, HALF), ds(n % 2, CN)] = value

    def kept_total(n):
        return intra[n // 4, ds(n // 2 % 2, HALF), ds(n % 2, CN)]

    def fin3(lane, j):
        n = lane * NH + j
        keep_total(n, summed(3, lane, j))

    def step(phase, lane, j):
        n = (1 - lane) * NH + j if phase == 1 else lane * NH + j
        if phase == 0:
            rb = zo
        elif phase == 3:
            rb = z
        else:
            rb = zr if lane == 0 else zl
        return product(phase, lane, j, rb, n)

    fins = (fin0, fin1, fin2, fin3)
    pending = None
    for phase in range(4):
        if phase == 0:
            square = finish(zo, first=True)
            all_of(w_v, once_sem.at[4])
        elif phase == 1:
            send_squares(zo, square)
            for rb in (zr, zl):
                inside(rb)
                gating(rb)
                send_squares(rb, finish(rb))
        elif phase == 3:
            inside(z)
            gating(z)
            send_squares(z, finish(z))
        for lane in range(2):
            r = step(phase, lane, 0)
            if pending is not None:
                pending(lane, NH - 1)
            own[lane] = r

        def body(j, _, phase=phase):
            for lane in range(2):
                r = step(phase, lane, j)
                fins[phase](lane, j - 1)
                own[lane] = r
            return 0

        lax.fori_loop(1, NH, body, 0)
        pending = fins[phase]
    for lane in range(2):
        pending(lane, NH - 1)

    all_of(ssq_in.at[0:N_HEAD - 1], scan_sem.at[4])
    squares = jnp.sum(ssq_in[...], axis=0)
    scale_row = lax.rsqrt(squares[0:1, :] * (1.0 / (HEADS * HD)) + EPS)
    scale = jnp.sum(
        jnp.where(r2 == c2, jnp.broadcast_to(scale_row, (HALF, HALF)), 0.0), axis=1, keepdims=True)

    all_of(near_in.at[0, NH:NC], early_rsem.at[0])
    all_of(near_in.at[1, 0:NH], early_rsem.at[1])

    def result(j, _):
        for lane in range(2):
            n = lane * NH + j
            near_copy(lane, n, right, late_rsem.at[lane, j]).wait_recv()
            s = kept_total(n) + near_in[0, n].astype(F32) + near_in[1, n].astype(F32)
            out_ref[:, ds(n, CN)] = (s * scale).astype(BF16)
        return 0

    lax.fori_loop(0, NH, result, 0)

    all_of(scan_out.at[0:N_CTX - 1], scan_sem.at[0])
    all_of(prefix_out.at[0:N_CTX - 2], scan_sem.at[2])

    @pl.when(ctx == 0)
    def _():
        all_of(prefix_out.at[0:1], scan_sem.at[2])

    all_of(ssq_out.at[0:N_HEAD - 1], scan_sem.at[3])
    all_of(core_out, core_ssem)
    all_of(z_out, z_ssem)


def shards(queries, keys, values, gate_logits, log_decay, norm_gain_vector, out_weight):
    any_spec = pl.BlockSpec(memory_space=pl.ANY)
    vmem = pl.BlockSpec(memory_space=pltpu.VMEM)
    dma = pltpu.SemaphoreType.DMA
    return pl.pallas_call(
        kernel,
        out_shape=pltpu.VMEM((ROWS // N_HEAD, D), BF16),
        in_specs=[any_spec] * 7,
        out_specs=vmem,
        scratch_shapes=[
            pltpu.VMEM((LH, ROWS), F32),
            pltpu.VMEM((1, WIDTH), F32),
            pltpu.VMEM((ROWS, WIDTH), BF16),
            pltpu.VMEM((ROWS, WIDTH), BF16),
            pltpu.VMEM((ROWS, WIDTH), BF16),
            pltpu.VMEM((ROWS, WIDTH), BF16),
            pltpu.VMEM((NC, WIDTH, CN), BF16),
            pltpu.VMEM((NB, BLOCK, WIDTH), BF16),
            pltpu.VMEM((NB, BLOCK, WIDTH), F32),
            pltpu.VMEM((NB, BLOCK, WIDTH), F32),
            pltpu.VMEM((NB, 4, 2, HD, HD), F32),
            pltpu.VMEM((NB, LH, BLOCK), F32),
            pltpu.VMEM((NB, BLOCK, LH), F32),
            pltpu.VMEM((NB, 4, 2, HD), F32),
            pltpu.VMEM((NB, 4, 2, BLOCK), F32),
            pltpu.VMEM((NB, 4, 2, HD), F32),
            pltpu.VMEM((4, 2, 16, HD), BF16),
            pltpu.VMEM((N_CTX, MSG, HD), BF16),
            pltpu.VMEM((N_CTX, MSG, HD), BF16),
            pltpu.VMEM((N_CTX, SL, HD), BF16),
            pltpu.VMEM((N_CTX, SL, HD), BF16),
            pltpu.VMEM((N_HEAD, 8, HALF), F32),
            pltpu.VMEM((N_HEAD, 8, HALF), F32),
            pltpu.VMEM((4 * NC, HALF, CN), BF16),
            pltpu.VMEM((4 * NC, HALF, CN), BF16),
            pltpu.VMEM((2, HALF, CN), F32),
            pltpu.VMEM((3, NC, HALF, CN), BF16),
            pltpu.VMEM((NC, HALF, CN), BF16),
            pltpu.VMEM((2, NC, HALF, CN), BF16),
            dma((2, NB)), dma((5,)), dma((5,)), dma((4,)), dma((4,)),
            dma, dma((2, 4)),
            dma, dma((NC // 2,)), dma((2,)), dma((2, NH)),
        ],
        compiler_params=pltpu.CompilerParams(
            collective_id=0, has_side_effects=True, vmem_limit_bytes=60 * 1024 * 1024),
        cost_estimate=pl.CostEstimate(
            flops=15_000_000_000, bytes_accessed=23_000_000, transcendentals=4_000_000),
        name="attention",
    )(queries, keys, values, gate_logits, log_decay, norm_gain_vector.reshape(1, WIDTH), out_weight)


def solution(mesh):
    in_specs = (
        P("ctx", "head"),
        P("ctx", "head"),
        P("ctx", "head"),
        P("ctx", "head"),
        P("head", "ctx"),
        P("head"),
        P("head", None),
    )
    out_specs = P(("ctx", "head"), None)
    return jax.shard_map(shards, mesh=mesh, in_specs=in_specs, out_specs=out_specs, check_vma=False)
```
